32 devices in a mesh: groups: 2 (over y), wide: 4 (over z), narrow: 4 (over x, core).
Axes of the slice: x: 2, y: 2, z: 4, core: 2. Of those that a mesh axis runs over, the one named last changes fastest.
Arguments:
- environment: float32 [10, 4096, 4096], P('groups', 'wide', 'narrow'), parts along dimension 0, may hold values from -6 to 6
- ket_site: float32 [8192, 2, 512], P(('groups', 'narrow'), None, 'wide'), parts along dimension 0, may hold values from -0.0625 to 0.0625
- bra_site: float32 [8192, 2, 4096], P(('groups', 'wide'), None, 'narrow'), parts along dimension 0, may hold values from -0.0625 to 0.0625
- mpo_table: float32 [16, 5, 5, 2, 2], replicated
- field_index: int32 [2], P('groups'), parts along dimension 0, may hold values from 0 to 15
- owners: int32 [4], P('groups'), parts along dimension 0, may hold values from 0 to 3
Outputs:
- new_panels: float32 [4, 5, 4096, 128], P('groups', None, 'narrow', 'wide'), parts along dimension 0
The draws below stay inside these ranges and needn't reach their ends.
There are 2 independent parts, one for each index of `groups`. The reference program is written for one: setup_inputs(seed, part) draws one part's arguments, and reference() takes and returns one part's arrays. A program takes and returns all parts, laid end to end along the dimension named above; an argument that names none is the same for every part. Nothing has to cross between parts.
All inputs are finite; a program needn't handle non-finite values.
Results may differ from the reference program's by a relative error of at most 0.0001.
Values sent between devices are 32-bit elements; how exact they have to be, the bound alone decides.
A program may use at most 128 MiB of HBM per device.

```python
import jax
import jax.numpy as jnp
from jax import lax

CHI = 4096
BOND = 5
PHYS = 2
PANEL = 128
PANELS = 2
PATTERNS = 16
KET_COLS = 512
N_WIDE = 4


def draw_mpo_table(key, part):
    key = jax.random.fold_in(key, 7)
    key_field, key_coupling, key_aniso = jax.random.split(key, 3)
    fields = jax.random.uniform(key_field, (PATTERNS,), jnp.float32, -3.0, 3.0)
    coupling = jax.random.uniform(key_coupling, (PATTERNS,), jnp.float32, 0.5, 1.5)
    aniso = jax.random.uniform(key_aniso, (PATTERNS,), jnp.float32, 0.5, 1.5)
    identity_op = jnp.eye(2, dtype=jnp.float32)
    raise_op = jnp.array([[0.0, 1.0], [0.0, 0.0]], jnp.float32)
    lower_op = raise_op.T
    spin_z = jnp.array([[0.5, 0.0], [0.0, -0.5]], jnp.float32)
    ones = jnp.ones((PATTERNS, 1, 1), jnp.float32)
    table = jnp.zeros((PATTERNS, 5, 5, 2, 2), jnp.float32)
    table = table.at[:, 0, 0].set(ones * identity_op)
    table = table.at[:, 1, 0].set(ones * raise_op)
    table = table.at[:, 2, 0].set(ones * lower_op)
    table = table.at[:, 3, 0].set(ones * spin_z)
    table = table.at[:, 4, 0].set(fields[:, None, None] * spin_z)
    table = table.at[:, 4, 1].set(0.5 * coupling[:, None, None] * lower_op)
    table = table.at[:, 4, 2].set(0.5 * coupling[:, None, None] * raise_op)
    table = table.at[:, 4, 3].set(aniso[:, None, None] * spin_z)
    table = table.at[:, 4, 4].set(ones * identity_op)
    return table.astype(jnp.float32)


def block_levels(stream_key, dims, cuts, smallest, top_value):
    loudness = 1.0
    for position, blocks in cuts:
        steps = jax.random.uniform(jax.random.fold_in(jax.random.fold_in(stream_key, 6), position), (blocks,), jnp.float32, smallest / len(cuts), top_value / len(cuts))
        loudness = loudness * jnp.repeat(jnp.exp(steps), dims[position] // blocks).reshape((-1,) + (1,) * (len(dims) - 1 - position))
    return loudness


def centred(key, extent, width, reach, cuts=(), kind=jnp.bfloat16):
    level = block_levels(key, extent, cuts, -0.22, 0.18) if cuts else 1.0
    drawn = jax.random.normal(key, extent, jnp.float32) * width * level
    return jnp.minimum(jnp.maximum(drawn, -reach), reach).astype(kind)


def setup_inputs(seed: int = 0, part: int = 0) -> dict:
    streams_of = jax.random.split(jax.random.key(seed), 7)
    part_keys = jax.random.split(jax.random.fold_in(streams_of[6], part), 7)
    return {
        "environment": centred(part_keys[0], (BOND, CHI, CHI), 1.0, 6.0, ((1, 4), (2, 4)), jnp.float32),
        "ket_site": centred(part_keys[1], (CHI, PHYS, KET_COLS), (2 * CHI) ** -0.5, 0.0625, ((0, 4), (2, 4)), jnp.float32),
        "bra_site": centred(part_keys[2], (CHI, PHYS, CHI), (2 * CHI) ** -0.5, 0.0625, ((0, 4), (2, 4)), jnp.float32),
        "mpo_table": draw_mpo_table(jax.random.fold_in(streams_of[6], 71), part),
        "field_index": jax.random.randint(part_keys[4], (1,), 0, PATTERNS).astype(jnp.int32),
        "owners": jax.random.randint(part_keys[5], (PANELS,), 0, N_WIDE).astype(jnp.int32),
    }


precise = lax.Precision.HIGHEST


def select_mpo(mpo_table, field_index):
    patterns = jnp.arange(mpo_table.shape[0], dtype=jnp.int32)
    picked = (patterns == field_index[0].astype(jnp.int32)).astype(jnp.float32)
    return jnp.einsum('k,kwvst->wvst', picked, mpo_table, precision=precise)


def reference(environment, ket_site, bra_site, mpo_table, field_index, owners):
    local_mpo = select_mpo(mpo_table, field_index)
    blocks = []
    for number in range(PANELS):
        offset = (owners[number] * PANEL).astype(jnp.int32)
        columns = lax.dynamic_slice_in_dim(ket_site, offset, PANEL, 2)
        contracted = jnp.einsum('wab,btc->watc', environment, columns, precision=precise)
        applied = jnp.einsum('wvst,watc->vasc', local_mpo, contracted, precision=precise)
        blocks.append(jnp.einsum('asj,vasc->vjc', bra_site, applied, precision=precise))
    return jnp.stack(blocks)
```

```python
import functools

import jax
import jax.numpy as jnp
from jax import lax
from jax.experimental import pallas as pl
from jax.experimental.pallas import tpu as pltpu
from jax.sharding import PartitionSpec as P

PANELS = 2
LINE = 4
PIECES = 8
TILE = 256

precise = lax.Precision.HIGHEST


def spread(block, axis, source):
    block = jnp.where(lax.axis_index(axis) == source, block, jnp.zeros_like(block))
    return lax.psum(block, axis)


def select_mpo(mpo_table, field_index):
    patterns = jnp.arange(mpo_table.shape[0], dtype=jnp.int32)
    picked = (patterns == field_index[0]).astype(jnp.float32)
    return jnp.einsum("k,kwvst->wvst", picked, mpo_table, precision=precise)


def with_collectives(environment, ket_site, bra_site, mpo_table, field_index, owners):
    local_mpo = select_mpo(mpo_table, field_index)
    results = []
    for number in range(PANELS):
        summed = lax.psum(
            jnp.einsum(
                "wab,btc->watc",
                environment,
                spread(ket_site, "wide", owners[number]),
                precision=precise,
            ),
            "narrow",
        )
        applied = jnp.einsum("wvst,watc->vasc", local_mpo, summed, precision=precise)
        results.append(
            lax.psum_scatter(
                jnp.einsum("asj,vasc->vjc", bra_site, applied, precision=precise),
                "wide",
                scatter_dimension=2,
                tiled=True,
            )
        )
    return jnp.stack(results)


def halves(x):
    high = x.astype(jnp.bfloat16)
    return high, (x - high.astype(jnp.float32)).astype(jnp.bfloat16)


def times(a, b, b_dim):
    return lax.dot_general(
        a, b, (((1,), (b_dim,)), ((), ())), preferred_element_type=jnp.float32
    )


def kernel(
    bond, phys,
    ket, env, bra, mpo, owners, out,
    stage, bra_high, bra_low, stream, ket_parts, partial, from_core, applied, from_x, from_sibling, parts, product, from_z,
    load_sem, hop_send, hop_recv, core_send, core_recv, x_send, x_recv, share_send, share_recv, z_send, z_recv,
):
    group, z, n = lax.axis_index("groups"), lax.axis_index("wide"), lax.axis_index("narrow")
    x, core = n // 2, n % 2
    sibling, across = x * 2 + 1 - core, (1 - x) * 2 + core
    rows, depth = ket.shape
    panel = rows // phys
    half = panel // 2
    piece_rows = rows // PIECES
    piece = panel // LINE
    chunks = PANELS * bond
    width = bra_high.shape[2]
    high_rows = env.shape[1]

    def remote(src, dst, send, recv, at_z, at_n):
        return pltpu.make_async_remote_copy(
            src_ref=src, dst_ref=dst, send_sem=send, recv_sem=recv,
            device_id=(group, at_z, at_n), device_id_type=pl.DeviceIdType.MESH,
        )

    barrier = pltpu.get_barrier_semaphore()
    others = [(z, sibling), (z, across)] + [((z + d) % LINE, n) for d in range(1, LINE)]
    for at_z, at_n in others:
        pl.semaphore_signal(barrier, inc=1, device_id=(group, at_z, at_n), device_id_type=pl.DeviceIdType.MESH)
    pl.semaphore_wait(barrier, len(others))

    near = z // 2
    far = 1 - near

    def hop_copy(way, q):
        place = stream.at[way, q]
        return remote(place, place, hop_send.at[way, q], hop_recv.at[way, q], (z + 1 - 2 * way + LINE) % LINE, n)

    def hop(way, q):
        position = z + way * (LINE - 1 - 2 * z)
        mine = ket[pl.ds(pl.multiple_of((q % PIECES) * piece_rows, piece_rows), piece_rows), :]

        @pl.when(position == 0)
        def _():
            stream[way, q] = mine

        @pl.when(position > 0)
        def _():
            hop_copy(way, q).wait_recv()
            owned = owners[q // PIECES] == z
            stream[way, q] = jnp.where(owned, mine, stream[way, q])

        @pl.when(position < LINE - 1)
        def _():
            hop_copy(way, q).start()

    def hop_done(way, q):
        position = z + way * (LINE - 1 - 2 * z)

        @pl.when(position < LINE - 1)
        def _():
            hop_copy(way, q).wait_send()

    middle = (z == 1) | (z == 2)
    total = PANELS * PIECES

    def load(block, slot):
        return pltpu.make_async_copy(block, stage.at[slot], load_sem.at[slot])

    def load_env(w):
        return load(env.at[w], w % 2)

    load_env(0).start()
    load_env(1).start()

    @pl.when(jnp.logical_not(middle))
    def _():
        @pl.loop(0, total)
        def _(q):
            hop(near, q)

    @pl.when(middle)
    def _():
        hop(near, 0)

    def both(q):
        @pl.when(middle & (q + 1 < total))
        def _():
            hop(near, q + 1)

        hop(far, q)

    @pl.loop(0, PIECES)
    def _(q):
        both(q)

    def take_panel(p):
        owner_below = owners[p] <= z

        @pl.loop(0, PIECES)
        def _(i):
            q = p * PIECES + i
            high, low = halves(jnp.where(owner_below, stream[0, q], stream[1, q]))
            at = pl.multiple_of(i * piece_rows, piece_rows)
            ket_parts[p, pl.ds(at, piece_rows), :] = high
            ket_parts[p, pl.ds(pl.multiple_of(rows + at, piece_rows), piece_rows), :] = low

    def core_copy(p, w):
        return remote(
            partial.at[w, 1 - core], from_core.at[p, w], core_send.at[p, w], core_recv.at[p, w], z, sibling
        )

    def contract(p, w):
        load_env(w).wait()

        @pl.loop(0, high_rows // TILE)
        def _(tile):
            at = pl.multiple_of(tile * TILE, TILE)
            high, low = halves(stage[w % 2, pl.ds(at, TILE), :])
            wide = times(ket_parts[p], high, 1)
            result = wide[:rows] + wide[rows:] + times(ket_parts[p, :rows, :], low, 1)
            for t in range(phys):
                for k in range(2):
                    first = t * panel + k * half
                    partial[w, k, t, :, pl.ds(at, TILE)] = result[first:first + half]

        core_copy(p, w).start()

    take_panel(0)

    @pl.loop(0, bond)
    def _(w):
        contract(0, w)

        @pl.when(w + 2 < bond)
        def _():
            load_env(w + 2).start()

        both(PIECES + w)

    for s in range(phys):
        load(bra.at[:, s, :], s).start()

    def x_copy(k):
        return remote(applied.at[k], from_x.at[k], x_send.at[k], x_recv.at[k], z, across)

    def share_copy(k):
        return remote(applied.at[k], from_sibling.at[k], share_send.at[k], share_recv.at[k], z, sibling)

    def apply_mpo(p, started):
        @pl.loop(0, bond)
        def _(w):
            core_copy(p, w).wait_recv()
            partial[w, core] = partial[w, core] + from_core[p, w]

        @pl.loop(0, bond)
        def _(v):
            @pl.loop(0, half // 8)
            def _(r):
                at = pl.ds(pl.multiple_of(r * 8, 8), 8)
                given = [[partial[w, core, t, at, :] for t in range(phys)] for w in range(bond)]
                for s in range(phys):
                    value = None
                    for w in range(bond):
                        for t in range(phys):
                            term = mpo[((w * bond + v) * phys + s) * phys + t] * given[w][t]
                            value = term if value is None else value + term
                    applied[p * bond + v, s, at, :] = value

            @pl.when(v < started)
            def _():
                x_copy(p * bond + v).start()

        @pl.loop(0, bond)
        def _(w):
            core_copy(p, w).wait_send()

    apply_mpo(0, 2)

    @pl.loop(PIECES + bond, total)
    def _(q):
        both(q)

    take_panel(1)

    for s in range(phys):
        load(bra.at[:, s, :], s).wait()

        @pl.loop(0, high_rows // TILE)
        def _(tile, s=s):
            at = pl.ds(pl.multiple_of(tile * TILE, TILE), TILE)
            high, low = halves(stage[s, at, :])
            bra_high[s, at, :] = high
            bra_low[s, at, :] = low

    load_env(0).start()
    load_env(1).start()

    def sum_narrow(k):
        x_copy(k).wait()
        applied[k] = applied[k] + from_x[k]
        share_copy(k).start()

    def z_copy(k, d):
        at = (z + d) % LINE
        return remote(
            product.at[k % 2, pl.ds(pl.multiple_of(at * piece, piece), piece), :],
            from_z.at[k, d - 1], z_send.at[k, d - 1], z_recv.at[k, d - 1], at, n,
        )

    def place(source, k, side):
        for s in range(phys):
            high, low = halves(source[k, s])
            at = pl.multiple_of(side * half, half)
            parts[s, pl.ds(at, half), :] = high
            parts[s, pl.ds(pl.multiple_of(panel + at, half), half), :] = low

    def multiply(k):
        place(applied, k, core)
        share_copy(k).wait_recv()
        place(from_sibling, k, 1 - core)

        @pl.when(k >= 2)
        def _():
            for d in range(1, LINE):
                z_copy(k - 2, d).wait_send()

        @pl.loop(0, width // TILE)
        def _(tile):
            at = pl.ds(pl.multiple_of(tile * TILE, TILE), TILE)
            result = None
            for s in range(phys):
                wide = times(parts[s], bra_high[s, :, at], 0)
                term = wide[:panel] + wide[panel:] + times(parts[s, :panel, :], bra_low[s, :, at], 0)
                result = term if result is None else result + term
            product[k % 2, :, at] = result

        for d in range(1, LINE):
            z_copy(k, d).start()
        out[k] = product[k % 2, pl.ds(pl.multiple_of(z * piece, piece), piece), :]

    early = (bond + 1) // 2

    @pl.loop(0, early)
    def _(k):
        sum_narrow(k)

        @pl.when(k + 2 < bond)
        def _():
            x_copy(k + 2).start()

        multiply(k)
        for i in range(2):
            w = 2 * k + i

            @pl.when(w < bond)
            def _():
                contract(1, w)

                @pl.when(w + 2 < bond)
                def _():
                    load_env(w + 2).start()

    apply_mpo(1, 0)

    @pl.loop(early, chunks)
    def _(k):
        sum_narrow(k)

        @pl.when(k + 2 < chunks)
        def _():
            x_copy(k + 2).start()

        multiply(k)

    @pl.loop(0, chunks)
    def _(k):
        for d in range(1, LINE):
            z_copy(k, d).wait_recv()
        out[k] = (out[k] + from_z[k, 0]) + (from_z[k, 1] + from_z[k, 2])
        share_copy(k).wait_send()

    for k in (chunks - 2, chunks - 1):
        for d in range(1, LINE):
            z_copy(k, d).wait_send()

    @pl.loop(0, total)
    def _(q):
        hop_done(0, q)
        hop_done(1, q)


def in_kernel(environment, ket_site, bra_site, mpo_table, field_index, owners):
    bond, rows, depth = environment.shape
    phys, panel = ket_site.shape[1:]
    width = bra_site.shape[2]
    half, piece, chunks = panel // 2, panel // LINE, PANELS * bond
    mpo = select_mpo(mpo_table, field_index).reshape(-1)
    ket = ket_site.transpose(1, 2, 0).reshape(phys * panel, depth)
    dma, f32, bf16 = pltpu.SemaphoreType.DMA, jnp.float32, jnp.bfloat16
    vmem = pl.BlockSpec(memory_space=pltpu.VMEM)
    smem = pl.BlockSpec(memory_space=pltpu.SMEM)
    hbm = pl.BlockSpec(memory_space=pl.ANY)
    total = PANELS * PIECES
    result = pl.pallas_call(
        functools.partial(kernel, bond, phys),
        out_shape=jax.ShapeDtypeStruct((chunks, piece, width), f32),
        in_specs=[vmem, hbm, hbm, smem, smem],
        out_specs=vmem,
        scratch_shapes=[
            pltpu.VMEM((2, rows, depth), f32),
            pltpu.VMEM((phys, rows, width), bf16),
            pltpu.VMEM((phys, rows, width), bf16),
            pltpu.VMEM((2, total, phys * panel // PIECES, depth), f32),
            pltpu.VMEM((PANELS, 2 * phys * panel, depth), bf16),
            pltpu.VMEM((bond, 2, phys, half, rows), f32),
            pltpu.VMEM((PANELS, bond, phys, half, rows), f32),
            pltpu.VMEM((chunks, phys, half, rows), f32),
            pltpu.VMEM((chunks, phys, half, rows), f32),
            pltpu.VMEM((chunks, phys, half, rows), f32),
            pltpu.VMEM((phys, 2 * panel, rows), bf16),
            pltpu.VMEM((2, panel, width), f32),
            pltpu.VMEM((chunks, LINE - 1, piece, width), f32),
            dma((2,)),
            dma((2, total)), dma((2, total)),
            dma((PANELS, bond)), dma((PANELS, bond)),
            dma((chunks,)), dma((chunks,)),
            dma((chunks,)), dma((chunks,)),
            dma((chunks, LINE - 1)), dma((chunks, LINE - 1)),
        ],
        compiler_params=pltpu.CompilerParams(
            collective_id=0, has_side_effects=True, vmem_limit_bytes=62 * 2**20
        ),
    )(ket, environment, bra_site, mpo, owners)
    return result.reshape(PANELS, bond, piece, width).swapaxes(2, 3)


def solution(mesh):
    placed = (
        P("groups", "wide", "narrow"),
        P(("groups", "narrow"), None, "wide"),
        P(("groups", "wide"), None, "narrow"),
        P(),
        P("groups"),
        P("groups"),
    )
    fits = mesh.shape["wide"] == LINE and mesh.shape["narrow"] == 4
    return jax.shard_map(
        in_kernel if fits else with_collectives,
        mesh=mesh,
        in_specs=placed,
        out_specs=P("groups", None, "narrow", "wide"),
        check_vma=False,
    )
```

```python
import functools

import jax
import jax.numpy as jnp
from jax import lax
from jax.experimental import pallas as pl
from jax.experimental.pallas import tpu as pltpu
from jax.sharding import PartitionSpec as P

PANELS = 2
LINE = 4
SPLIT = 2
PIECES = 4
TILE = 256
AHEAD = 4
SLOTS = 4

precise = lax.Precision.HIGHEST


def spread(block, axis, source):
    block = jnp.where(lax.axis_index(axis) == source, block, jnp.zeros_like(block))
    return lax.psum(block, axis)


def select_mpo(mpo_table, field_index):
    patterns = jnp.arange(mpo_table.shape[0], dtype=jnp.int32)
    picked = (patterns == field_index[0]).astype(jnp.float32)
    return jnp.einsum("k,kwvst->wvst", picked, mpo_table, precision=precise)


def with_collectives(environment, ket_site, bra_site, mpo_table, field_index, owners):
    local_mpo = select_mpo(mpo_table, field_index)
    results = []
    for number in range(PANELS):
        summed = lax.psum(
            jnp.einsum(
                "wab,btc->watc",
                environment,
                spread(ket_site, "wide", owners[number]),
                precision=precise,
            ),
            "narrow",
        )
        applied = jnp.einsum("wvst,watc->vasc", local_mpo, summed, precision=precise)
        results.append(
            lax.psum_scatter(
                jnp.einsum("asj,vasc->vjc", bra_site, applied, precision=precise),
                "wide",
                scatter_dimension=2,
                tiled=True,
            )
        )
    return jnp.stack(results)


def halves(x):
    high = x.astype(jnp.bfloat16)
    return high, (x - high.astype(jnp.float32)).astype(jnp.bfloat16)


def times(a, b, b_dim):
    return lax.dot_general(
        a, b, (((1,), (b_dim,)), ((), ())), preferred_element_type=jnp.float32
    )


def kernel(
    bond, phys,
    ket, env, bra, mpo, owners, out,
    stage, bra_high, bra_low, stream, ket_parts, partial, from_core, applied, from_x, from_sibling, parts, product, from_z,
    load_sem, hop_send, hop_recv, core_send, core_recv, x_send, x_recv, share_send, share_recv, z_send, z_recv,
):
    group, z, n = lax.axis_index("groups"), lax.axis_index("wide"), lax.axis_index("narrow")
    x, core = n // 2, n % 2
    sibling, across = x * 2 + 1 - core, (1 - x) * 2 + core
    rows, depth = ket.shape[0] // SPLIT, ket.shape[1]
    panel = rows // phys
    units = PANELS * SPLIT
    half = panel // 2
    piece_rows = rows // PIECES
    piece = panel // LINE
    chunks = units * bond
    width = bra_high.shape[2]
    high_rows = env.shape[1]

    def remote(src, dst, send, recv, at_z, at_n):
        return pltpu.make_async_remote_copy(
            src_ref=src, dst_ref=dst, send_sem=send, recv_sem=recv,
            device_id=(group, at_z, at_n), device_id_type=pl.DeviceIdType.MESH,
        )

    barrier = pltpu.get_barrier_semaphore()
    others = [(z, sibling), (z, across)] + [((z + d) % LINE, n) for d in range(1, LINE)]
    for at_z, at_n in others:
        pl.semaphore_signal(barrier, inc=1, device_id=(group, at_z, at_n), device_id_type=pl.DeviceIdType.MESH)
    pl.semaphore_wait(barrier, len(others))

    near = z // 2
    far = 1 - near

    def hop_copy(way, q):
        place = stream.at[way, q]
        return remote(place, place, hop_send.at[way, q], hop_recv.at[way, q], (z + 1 - 2 * way + LINE) % LINE, n)

    def hop(way, q):
        position = z + way * (LINE - 1 - 2 * z)
        mine = ket[pl.ds(pl.multiple_of((q % (SPLIT * PIECES)) * piece_rows, piece_rows), piece_rows), :]

        @pl.when(position == 0)
        def _():
            stream[way, q] = mine

        @pl.when(position > 0)
        def _():
            hop_copy(way, q).wait_recv()
            owned = owners[q // (SPLIT * PIECES)] == z
            stream[way, q] = jnp.where(owned, mine, stream[way, q])

        @pl.when(position < LINE - 1)
        def _():
            hop_copy(way, q).start()

    def hop_done(way, q):
        position = z + way * (LINE - 1 - 2 * z)

        @pl.when(position < LINE - 1)
        def _():
            hop_copy(way, q).wait_send()

    middle = (z == 1) | (z == 2)
    total = units * PIECES

    def load(block, slot):
        return pltpu.make_async_copy(block, stage.at[slot], load_sem.at[slot])

    def load_env(w):
        return load(env.at[w], w % 2)

    load_env(0).start()
    load_env(1).start()

    @pl.when(jnp.logical_not(middle))
    def _():
        @pl.loop(0, total)
        def _(q):
            hop(near, q)

    @pl.when(middle)
    def _():
        hop(near, 0)

    def both(q):
        @pl.when(middle & (q + 1 < total))
        def _():
            hop(near, q + 1)

        hop(far, q)

    @pl.loop(0, PIECES)
    def _(q):
        both(q)

    def take_panel(p):
        owner_below = owners[p // SPLIT] <= z

        @pl.loop(0, PIECES)
        def _(i):
            q = p * PIECES + i
            high, low = halves(jnp.where(owner_below, stream[0, q], stream[1, q]))
            at = pl.multiple_of(i * piece_rows, piece_rows)
            ket_parts[p, pl.ds(at, piece_rows), :] = high
            ket_parts[p, pl.ds(pl.multiple_of(rows + at, piece_rows), piece_rows), :] = low

    def core_copy(p, w):
        return remote(
            partial.at[w, 1 - core], from_core.at[p, w], core_send.at[p, w], core_recv.at[p, w], z, sibling
        )

    def contract(p, w):
        load_env(w).wait()

        @pl.loop(0, high_rows // TILE)
        def _(tile):
            at = pl.multiple_of(tile * TILE, TILE)
            high, low = halves(stage[w % 2, pl.ds(at, TILE), :])
            wide = times(ket_parts[p], high, 1)
            result = wide[:rows] + wide[rows:] + times(ket_parts[p, :rows, :], low, 1)
            for t in range(phys):
                for k in range(2):
                    first = t * panel + k * half
                    partial[w, k, t, :, pl.ds(at, TILE)] = result[first:first + half]

        core_copy(p, w).start()

    take_panel(0)

    @pl.loop(0, bond)
    def _(w):
        contract(0, w)

        @pl.when(w + 2 < bond)
        def _():
            load_env(w + 2).start()

        both(PIECES + w)

    for s in range(phys):
        load(bra.at[:, s, :], s).start()

    def x_copy(k):
        return remote(applied.at[k], from_x.at[k], x_send.at[k], x_recv.at[k], z, across)

    def share_copy(k):
        return remote(applied.at[k], from_sibling.at[k], share_send.at[k], share_recv.at[k], z, sibling)

    def apply_mpo(p, started):
        @pl.loop(0, bond)
        def _(w):
            core_copy(p, w).wait_recv()
            partial[w, core] = partial[w, core] + from_core[p, w]

        @pl.loop(0, bond)
        def _(v):
            @pl.loop(0, half // 8)
            def _(r):
                at = pl.ds(pl.multiple_of(r * 8, 8), 8)
                given = [[partial[w, core, t, at, :] for t in range(phys)] for w in range(bond)]
                for s in range(phys):
                    value = None
                    for w in range(bond):
                        for t in range(phys):
                            term = mpo[((w * bond + v) * phys + s) * phys + t] * given[w][t]
                            value = term if value is None else value + term
                    applied[p * bond + v, s, at, :] = value

            @pl.when(v < started)
            def _():
                x_copy(p * bond + v).start()

        @pl.loop(0, bond)
        def _(w):
            core_copy(p, w).wait_send()

    apply_mpo(0, AHEAD)

    @pl.loop(PIECES + bond, total)
    def _(q):
        both(q)

    for s in range(phys):
        load(bra.at[:, s, :], s).wait()

        @pl.loop(0, high_rows // TILE)
        def _(tile, s=s):
            at = pl.ds(pl.multiple_of(tile * TILE, TILE), TILE)
            high, low = halves(stage[s, at, :])
            bra_high[s, at, :] = high
            bra_low[s, at, :] = low

    load_env(0).start()
    load_env(1).start()

    def sum_narrow(k):
        x_copy(k).wait()
        applied[k] = applied[k] + from_x[k]
        share_copy(k).start()

    def z_copy(k, d):
        at = (z + d) % LINE
        return remote(
            product.at[k % SLOTS, pl.ds(pl.multiple_of(at * piece, piece), piece), :],
            from_z.at[k, d - 1], z_send.at[k, d - 1], z_recv.at[k, d - 1], at, n,
        )

    def place(source, k, side):
        for s in range(phys):
            high, low = halves(source[k, s])
            at = pl.multiple_of(side * half, half)
            parts[s, pl.ds(at, half), :] = high
            parts[s, pl.ds(pl.multiple_of(panel + at, half), half), :] = low

    def multiply(k):
        place(applied, k, core)
        share_copy(k).wait_recv()
        place(from_sibling, k, 1 - core)

        @pl.when(k >= SLOTS)
        def _():
            for d in range(1, LINE):
                z_copy(k - SLOTS, d).wait_send()

        @pl.loop(0, width // TILE)
        def _(tile):
            at = pl.ds(pl.multiple_of(tile * TILE, TILE), TILE)
            result = None
            for s in range(phys):
                wide = times(parts[s], bra_high[s, :, at], 0)
                term = wide[:panel] + wide[panel:] + times(parts[s, :panel, :], bra_low[s, :, at], 0)
                result = term if result is None else result + term
            product[k % SLOTS, :, at] = result

        for d in range(1, LINE):
            z_copy(k, d).start()
        out[k] = product[k % SLOTS, pl.ds(pl.multiple_of(z * piece, piece), piece), :]

    sum_narrow(0)

    @pl.loop(0, units)
    def _(u):
        more = u + 1 < units

        @pl.loop(0, bond)
        def _(i):
            k = u * bond + i
            last = i == bond - AHEAD

            @pl.when(k + 1 < chunks)
            def _():
                sum_narrow(k + 1)

            @pl.when((k + AHEAD < chunks) & jnp.logical_not(last))
            def _():
                x_copy(k + AHEAD).start()

            multiply(k)

            @pl.when(more & (i == 0))
            def _():
                take_panel(u + 1)

            @pl.loop(3 * i, 3 * i + 3)
            def _(w):
                @pl.when(more & (w < bond))
                def _():
                    contract(u + 1, w)

                    @pl.when(w + 2 < bond)
                    def _():
                        load_env(w + 2).start()

            @pl.when(more & last)
            def _():
                apply_mpo(u + 1, 0)

                @pl.when(u + 2 < units)
                def _():
                    load_env(0).start()
                    load_env(1).start()

            @pl.when((k + AHEAD < chunks) & last)
            def _():
                x_copy(k + AHEAD).start()

    @pl.loop(0, chunks)
    def _(k):
        for d in range(1, LINE):
            z_copy(k, d).wait_recv()
        out[k] = (out[k] + from_z[k, 0]) + (from_z[k, 1] + from_z[k, 2])
        share_copy(k).wait_send()

    for k in range(chunks - SLOTS, chunks):
        for d in range(1, LINE):
            z_copy(k, d).wait_send()

    @pl.loop(0, total)
    def _(q):
        hop_done(0, q)
        hop_done(1, q)


def in_kernel(environment, ket_site, bra_site, mpo_table, field_index, owners):
    bond, rows, depth = environment.shape
    phys, panel = ket_site.shape[1:]
    width = bra_site.shape[2]
    mpo = select_mpo(mpo_table, field_index).reshape(-1)
    small = panel // (LINE * SPLIT)
    ket = ket_site.reshape(depth, phys, LINE, SPLIT, small).transpose(3, 1, 2, 4, 0)
    ket = ket.reshape(phys * panel, depth)
    units, panel = PANELS * SPLIT, panel // SPLIT
    half, piece, chunks = panel // 2, panel // LINE, units * bond
    dma, f32, bf16 = pltpu.SemaphoreType.DMA, jnp.float32, jnp.bfloat16
    vmem = pl.BlockSpec(memory_space=pltpu.VMEM)
    smem = pl.BlockSpec(memory_space=pltpu.SMEM)
    hbm = pl.BlockSpec(memory_space=pl.ANY)
    total = units * PIECES
    result = pl.pallas_call(
        functools.partial(kernel, bond, phys),
        out_shape=jax.ShapeDtypeStruct((chunks, piece, width), f32),
        in_specs=[vmem, hbm, hbm, smem, smem],
        out_specs=vmem,
        scratch_shapes=[
            pltpu.VMEM((2, rows, depth), f32),
            pltpu.VMEM((phys, rows, width), bf16),
            pltpu.VMEM((phys, rows, width), bf16),
            pltpu.VMEM((2, total, phys * panel // PIECES, depth), f32),
            pltpu.VMEM((units, 2 * phys * panel, depth), bf16),
            pltpu.VMEM((bond, 2, phys, half, rows), f32),
            pltpu.VMEM((units, bond, phys, half, rows), f32),
            pltpu.VMEM((chunks, phys, half, rows), f32),
            pltpu.VMEM((chunks, phys, half, rows), f32),
            pltpu.VMEM((chunks, phys, half, rows), f32),
            pltpu.VMEM((phys, 2 * panel, rows), bf16),
            pltpu.VMEM((SLOTS, panel, width), f32),
            pltpu.VMEM((chunks, LINE - 1, piece, width), f32),
            dma((2,)),
            dma((2, total)), dma((2, total)),
            dma((units, bond)), dma((units, bond)),
            dma((chunks,)), dma((chunks,)),
            dma((chunks,)), dma((chunks,)),
            dma((chunks, LINE - 1)), dma((chunks, LINE - 1)),
        ],
        compiler_params=pltpu.CompilerParams(
            collective_id=0, has_side_effects=True, vmem_limit_bytes=62 * 2**20
        ),
    )(ket, environment, bra_site, mpo, owners)
    result = result.reshape(PANELS, SPLIT, bond, piece, width).transpose(0, 2, 4, 1, 3)
    return result.reshape(PANELS, bond, width, SPLIT * piece)


def solution(mesh):
    placed = (
        P("groups", "wide", "narrow"),
        P(("groups", "narrow"), None, "wide"),
        P(("groups", "wide"), None, "narrow"),
        P(),
        P("groups"),
        P("groups"),
    )
    fits = mesh.shape["wide"] == LINE and mesh.shape["narrow"] == 4
    return jax.shard_map(
        in_kernel if fits else with_collectives,
        mesh=mesh,
        in_specs=placed,
        out_specs=P("groups", None, "narrow", "wide"),
        check_vma=False,
    )
```
